256 devices in a mesh: dp: 32 (over x, z), fsdp: 4 (over y), tensor: 2 (over core).
Axes of the slice: x: 4, y: 4, z: 8, core: 2. Of those that a mesh axis runs over, the one named last changes fastest.
Arguments:
- activations: bfloat16 [32768, 8192], P(('dp', 'fsdp')), may hold values from -6 to 6
- out_grads: bfloat16 [32768, 2, 2048], P(('dp', 'fsdp'), 'tensor'), may hold values from -0.032958984 to 0.032958984
- basis: bfloat16 [8192, 1024], P('dp'), may hold values from -0.0625 to 0.0625
- weights: bfloat16 [2, 2048, 8192], P('tensor', ('dp', 'fsdp')), may hold values from -3 to 3
- first_moment: float32 [2, 2048, 1024], P('tensor', ('dp', 'fsdp')), may hold values from -2 to 2
- second_moment: float32 [2, 2048, 1024], P('tensor', ('dp', 'fsdp')), may hold values from 0.0001 to 0.01
Outputs:
- new_weights: bfloat16 [2, 2048, 8192], P('tensor', 'dp')
- first_new: float32 [2, 2048, 1024], P('tensor', ('dp', 'fsdp'))
- second_new: float32 [2, 2048, 1024], P('tensor', ('dp', 'fsdp'))
The draws below stay inside these ranges and needn't reach their ends.
All inputs are finite; a program needn't handle non-finite values.
Results may differ from the reference program's by a relative error of at most 0.012.
Values may be sent and summed in bfloat16 or wider, within the bound.
No kernel may reach another device: no remote copies, remote signals or barrier semaphores. Data moves between devices by JAX's collectives and lax.ppermute only.
A program may use at most 128 MiB of HBM per device.

```python
import math
import jax
import jax.numpy as jnp

D = 8192
RANK = 1024
STEP = 10
GROUPS = 2
HALF = 2048
TOKENS = 32768


def levels(stream_key, dims, split, low, high):
    def one(dim, blocks):
        heights = jax.random.uniform(jax.random.fold_in(jax.random.fold_in(stream_key, 6), dim), (blocks,), jnp.float32, low / len(split), high / len(split))
        return jnp.repeat(jnp.exp(heights), dims[dim] // blocks).reshape((-1,) + (1,) * (len(dims) - dim - 1))

    loudness = one(*split[0])
    for cut in split[1:]:
        loudness = loudness * one(*cut)
    return loudness


def centred(own_key, extent, deviation, most, cuts=(), dtype=jnp.bfloat16):
    array = deviation * jax.random.normal(own_key, extent, jnp.float32)
    if cuts:
        array = array * levels(own_key, extent, cuts, -0.22, 0.18)
    return jnp.clip(array, -most, most).astype(dtype)


def setup_inputs(seed: int = 0) -> dict:
    streams_of = jax.random.split(jax.random.key(seed), 7)
    activations = centred(streams_of[0], (TOKENS, D), 1.0, 6.0, ((0, 128),))
    out_grads = centred(streams_of[1], (TOKENS, GROUPS, HALF), (1.0 / TOKENS ** 0.5), 0.032958984, ((0, 128), (1, 2)))
    basis = centred(streams_of[2], (D, RANK), D ** -0.5, 0.0625, ((0, 32),))
    weights = centred(streams_of[3], (GROUPS, HALF, D), 0.5, 3.0, ((0, 2), (1, 128)))
    first_moment = centred(streams_of[4], (GROUPS, HALF, RANK), 0.3, 2.0, ((0, 2), (1, 128)), jnp.float32)
    second_moment = jnp.clip(jnp.exp(math.log(0.01) - 4.6051702 * jax.random.uniform(streams_of[5], (GROUPS, HALF, RANK), jnp.float32) ** levels(streams_of[5], (GROUPS, HALF, RANK), ((0, 2), (1, 128)), -0.2, 0.2)), 0.0001, 0.01)
    return dict(activations=activations, out_grads=out_grads, basis=basis, weights=weights, first_moment=first_moment, second_moment=second_moment)


beta_one = 0.9
beta_two = 0.999
epsilon = 1e-08
step_scale = 0.25

def reference(activations, out_grads, basis, weights, first_moment, second_moment):
    low_rank = jnp.dot(activations, basis, preferred_element_type=jnp.float32).astype(jnp.bfloat16)
    cotangent = out_grads.reshape(TOKENS, GROUPS * HALF)
    projected = jnp.dot(cotangent.T, low_rank, preferred_element_type=jnp.float32)
    projected = projected.reshape(GROUPS, HALF, RANK)
    first_new = beta_one * first_moment + (1.0 - beta_one) * projected
    second_new = beta_two * second_moment + (1.0 - beta_two) * projected * projected
    corrected = first_new / (1.0 - beta_one ** STEP)
    scaled = jnp.sqrt(second_new / (1.0 - beta_two ** STEP)) + epsilon
    direction = (corrected / scaled).astype(jnp.bfloat16)
    update = jnp.dot(direction.reshape(GROUPS * HALF, RANK), basis.T, preferred_element_type=jnp.float32)
    update = update.reshape(GROUPS, HALF, D)
    new_weights = (weights.astype(jnp.float32) - step_scale * update).astype(jnp.bfloat16)
    return (new_weights, first_new, second_new)
```

```python
import jax
import jax.numpy as jnp
from jax import lax
from jax.sharding import PartitionSpec as P

STEP = 10

beta_one = 0.9
beta_two = 0.999
epsilon = 1e-08
step_scale = 0.25

NX, NZ, NY = 4, 8, 4
f32 = jnp.float32
bf16 = jnp.bfloat16


def along_x(value, d):
    pairs = [(x * NZ + z, (x + d) % NX * NZ + z) for x in range(NX) for z in range(NZ)]
    return lax.ppermute(value, "dp", pairs)


def along_z(value, d):
    pairs = [(x * NZ + z, x * NZ + (z + d) % NZ) for x in range(NX) for z in range(NZ)]
    return lax.ppermute(value, "dp", pairs)


def along_y(value, d):
    return lax.ppermute(value, "fsdp", [(y, (y + d) % NY) for y in range(NY)])


def across(value):
    return lax.ppermute(value, "tensor", [(0, 1), (1, 0)])


def rows(array, start, size):
    return lax.dynamic_slice_in_dim(array, start, size, axis=0)


def columns(array, start, size):
    return lax.dynamic_slice_in_dim(array, start, size, axis=1)


def put(whole, part, start, axis):
    return lax.dynamic_update_slice_in_dim(whole, part, start, axis=axis)


def gather_z(block, z):
    n, h = block.shape[0], block.shape[0] // 2
    whole = jnp.zeros((NZ * n, block.shape[1]), block.dtype)
    whole = put(whole, block, z * n, 0)
    ahead = back = block
    for s in range(1, NZ // 2):
        ahead, back = along_z(ahead, 1), along_z(back, -1)
        whole = put(whole, ahead, lax.rem(z + NZ - s, NZ) * n, 0)
        whole = put(whole, back, lax.rem(z + s, NZ) * n, 0)
    far = lax.rem(z + NZ // 2, NZ) * n
    whole = put(whole, along_z(ahead[:h], 1), far, 0)
    return put(whole, along_z(back[h:], -1), far + h, 0)


def gather_y(block, y):
    n = block.shape[0]
    whole = jnp.zeros((NY * n, block.shape[1]), block.dtype)
    whole = put(whole, block, y * n, 0)
    for d in range(1, NY):
        whole = put(whole, along_y(block, d), lax.rem(y + NY - d, NY) * n, 0)
    return whole


def dot(a, b, dims):
    return lax.dot_general(a, b, ((dims[0], dims[1]), ((), ())), preferred_element_type=f32)


def shards(activations, out_grads, basis, weights, first_moment, second_moment):
    dp, y, core = lax.axis_index("dp"), lax.axis_index("fsdp"), lax.axis_index("tensor")
    x, z = lax.div(dp, NZ), lax.rem(dp, NZ)
    tokens, width = activations.shape
    rank = basis.shape[1]
    half, quarter, pair = rank // 2, width // NX, tokens // 2

    held = gather_z(columns(basis, core * half, half), z)

    mine = rows(activations, core * pair, pair)
    own = [columns(mine, x * quarter, quarter)]
    other = [columns(rows(activations, (1 - core) * pair, pair), x * quarter, quarter)]
    for d in range(1, NX):
        own.append(along_x(columns(mine, lax.rem(x + d, NX) * quarter, quarter), d))
        other.append(across(own[-1]))

    turned = out_grads[:, 0, :].T.reshape(NX * NZ, NY, 16, tokens)
    parts = []
    for d in range(NY):
        part = lax.dynamic_index_in_dim(turned, lax.rem(y + d, NY), axis=1, keepdims=False)
        parts.append(part if d == 0 else along_y(part, d))
    features = jnp.concatenate(parts, axis=2)
    crossed = across(features)
    first = core == 0
    features = jnp.stack(
        [jnp.where(first, features, crossed), jnp.where(first, crossed, features)], axis=1
    )

    weight_rows = gather_y(weights[0], y)

    near = dot(jnp.concatenate(own, axis=0), held, ((1,), (0,))).reshape(NX, pair, half)
    away = dot(jnp.concatenate(other, axis=0), held, ((1,), (0,))).reshape(NX, pair, half)
    partial = jnp.concatenate(
        [jnp.where(first, near, away), jnp.where(first, away, near)], axis=1
    )
    sent = partial.astype(bf16)
    total = partial[0]
    for d in range(1, NX):
        total = total + along_x(sent[d], -d).astype(f32)
    low_rank = total.astype(bf16)

    low_rank, held = lax.optimization_barrier((low_rank, held))
    low = jnp.concatenate([low_rank] + [along_y(low_rank, d) for d in range(1, NY)], axis=0)

    projected = dot(features.reshape(-1, NY * tokens), low, ((1,), (0,)))
    projected = projected.astype(bf16).reshape(2 * NX * NZ, 16, half)
    got = lax.all_to_all(projected, ("dp", "tensor"), split_axis=0, concat_axis=0, tiled=True)
    got = got.reshape(NX * NZ, 2, 16, half).astype(f32).sum(axis=0)
    projected = jnp.concatenate([got[0], got[1]], axis=1)[None]

    first_new = beta_one * first_moment + (1.0 - beta_one) * projected
    second_new = beta_two * second_moment + (1.0 - beta_two) * projected * projected
    corrected = first_new / (1.0 - beta_one**STEP)
    scaled = jnp.sqrt(second_new / (1.0 - beta_two**STEP)) + epsilon
    direction = gather_y((corrected / scaled).astype(bf16)[0], y)

    up, down = along_x(held, 1), along_x(held, -1)
    mid = held.shape[0] // 2
    far = jnp.concatenate([along_x(up[:mid], 1), along_x(down[mid:], -1)], axis=0)
    direction_own = columns(direction, core * half, half)
    direction_other = columns(direction, (1 - core) * half, half)
    new_weights = jnp.zeros_like(weight_rows)
    for d, part in ((0, held), (1, up), (3, down), (2, far)):
        update = dot(direction_own, part, ((1,), (1,)))
        update = update + dot(direction_other, across(part), ((1,), (1,)))
        place = lax.rem(x + NX - d, NX) * quarter
        old = columns(weight_rows, place, quarter).astype(f32)
        new_weights = put(new_weights, (old - step_scale * update).astype(bf16), place, 1)
    return (new_weights[None], first_new, second_new)


def solution(mesh):
    return jax.shard_map(
        shards,
        mesh=mesh,
        in_specs=(
            P(("dp", "fsdp"), None),
            P(("dp", "fsdp"), "tensor", None),
            P("dp", None),
            P("tensor", ("dp", "fsdp"), None),
            P("tensor", ("dp", "fsdp"), None),
            P("tensor", ("dp", "fsdp"), None),
        ),
        out_specs=(
            P("tensor", "dp", None),
            P("tensor", ("dp", "fsdp"), None),
            P("tensor", ("dp", "fsdp"), None),
        ),
        check_vma=False,
    )
```

```python
import jax
import jax.numpy as jnp
from jax import lax
from jax.experimental import pallas as pl
from jax.experimental.pallas import tpu as pltpu
from jax.sharding import PartitionSpec as P

STEP = 10

beta_one = 0.9
beta_two = 0.999
epsilon = 1e-08
step_scale = 0.25

NX, NZ, NY = 4, 8, 4
f32 = jnp.float32
bf16 = jnp.bfloat16


def along_x(value, d):
    pairs = [(x * NZ + z, (x + d) % NX * NZ + z) for x in range(NX) for z in range(NZ)]
    return lax.ppermute(value, "dp", pairs)


def along_z(value, d):
    pairs = [(x * NZ + z, x * NZ + (z + d) % NZ) for x in range(NX) for z in range(NZ)]
    return lax.ppermute(value, "dp", pairs)


def along_y(value, d):
    return lax.ppermute(value, "fsdp", [(y, (y + d) % NY) for y in range(NY)])


def across(value):
    return lax.ppermute(value, "tensor", [(0, 1), (1, 0)])


def fetch(value, sources):
    pairs = [
        (((x + sources[y % 2]) % NX * NZ + z) * NY + y, (x * NZ + z) * NY + y)
        for x in range(NX)
        for z in range(NZ)
        for y in range(NY)
    ]
    return lax.ppermute(value, ("dp", "fsdp"), pairs)


def rows(array, start, size):
    return lax.dynamic_slice_in_dim(array, start, size, axis=0)


def columns(array, start, size):
    return lax.dynamic_slice_in_dim(array, start, size, axis=1)


def put(whole, part, start, axis):
    return lax.dynamic_update_slice_in_dim(whole, part, start, axis=axis)


def gather_y(block, y):
    n = block.shape[0]
    whole = jnp.zeros((NY * n, block.shape[1]), block.dtype)
    whole = put(whole, block, y * n, 0)
    for d in range(1, NY):
        whole = put(whole, along_y(block, d), lax.rem(y + NY - d, NY) * n, 0)
    return whole


def dot(a, b, dims):
    return lax.dot_general(a, b, ((dims[0], dims[1]), ((), ())), preferred_element_type=f32)


def cut(activations, place):
    pair, quarter = activations.shape[0] // 2, activations.shape[1] // NX

    def kernel(place_ref, act_ref, *refs):
        outs, sems = refs[:-1], refs[-1]
        copies = []
        for n, out in enumerate(outs):
            row = pl.multiple_of(place_ref[0, n], pair)
            col = pl.multiple_of(place_ref[1, n], quarter)
            source = act_ref.at[pl.ds(row, pair), pl.ds(col, quarter)]
            copies.append(pltpu.make_async_copy(source, out, sems.at[n]))
        for copy in copies:
            copy.start()
        for copy in copies:
            copy.wait()

    shape = jax.ShapeDtypeStruct((pair, quarter), activations.dtype)
    return pl.pallas_call(
        kernel,
        out_shape=[shape] * (NX + 1),
        in_specs=[pl.BlockSpec(memory_space=pltpu.SMEM), pl.BlockSpec(memory_space=pl.ANY)],
        out_specs=[pl.BlockSpec(memory_space=pltpu.VMEM)] * (NX + 1),
        scratch_shapes=[pltpu.SemaphoreType.DMA((NX + 1,))],
    )(place, activations)


def shards(activations, out_grads, basis, weights, first_moment, second_moment):
    dp, y, core = lax.axis_index("dp"), lax.axis_index("fsdp"), lax.axis_index("tensor")
    x, z = lax.div(dp, NZ), lax.rem(dp, NZ)
    tokens, width = activations.shape
    rank = basis.shape[1]
    half, quarter, pair = rank // 2, width // NX, tokens // 2

    mine = columns(basis, core * half, half)
    n, h = mine.shape[0], mine.shape[0] // 2
    ahead, back = along_z(mine, 1), along_z(mine, -1)
    places = [(core, x), (1 - core, x)] + [(core, lax.rem(x + d, NX)) for d in range(1, NX)]
    place = jnp.stack(
        [jnp.stack([r * pair for r, _ in places]), jnp.stack([q * quarter for _, q in places])]
    )
    here, there, *leaving = cut(activations, place)
    ahead, back, *leaving = lax.optimization_barrier((ahead, back, *leaving))
    own, other = [here], [there]
    for d in range(1, NX):
        own.append(along_x(leaving[d - 1], d))

    held = jnp.zeros((NZ * n, half), bf16)
    held = put(held, mine, z * n, 0)
    for s in range(1, NZ // 2):
        if s > 1:
            ahead, back = along_z(ahead, 1), along_z(back, -1)
        held = put(held, ahead, lax.rem(z + NZ - s, NZ) * n, 0)
        held = put(held, back, lax.rem(z + s, NZ) * n, 0)
    back, out_grads = lax.optimization_barrier((back, out_grads))
    turned = out_grads[:, 0, :].T.reshape(NX * NZ, NY, 16, tokens)
    parts = []
    for d in range(NY):
        part = lax.dynamic_index_in_dim(turned, lax.rem(y + d, NY), axis=1, keepdims=False)
        parts.append(part if d == 0 else along_y(part, d))

    own, _, parts = lax.optimization_barrier((own, back, parts))

    far = lax.rem(z + NZ // 2, NZ) * n
    held = put(held, along_z(ahead[:h], 1), far, 0)
    held = put(held, along_z(back[h:], -1), far + h, 0)
    for d in range(1, NX):
        other.append(across(own[d]))

    odd = lax.rem(y, 2)
    span = [[lax.rem(x + o, NX) * quarter, lax.rem(x + o + 2, NX) * quarter] for o in (0, 1)]
    here_at = [jnp.where(odd == 1, q, p) for p, q in zip(*span)]
    there_at = [jnp.where(odd == 1, p, q) for p, q in zip(*span)]
    sources = ((0, 1), (2, 3))
    cuts = (0, quarter // 4, quarter)
    pieces = [held[i:j] for i, j in zip(cuts, cuts[1:])]
    slots = [[fetch(pieces[0], o)] for o in sources]

    first = core == 0
    near = dot(jnp.concatenate(own, axis=0), held, ((1,), (0,))).reshape(NX, pair, half)
    away = dot(jnp.concatenate(other, axis=0), held, ((1,), (0,))).reshape(NX, pair, half)
    partial = jnp.concatenate(
        [jnp.where(first, near, away), jnp.where(first, away, near)], axis=1
    )
    sent = partial.astype(bf16)
    sent, slots[0][0], slots[1][0] = lax.optimization_barrier((sent, slots[0][0], slots[1][0]))
    features = jnp.concatenate(parts, axis=2)
    crossed = across(features)
    features = jnp.stack(
        [jnp.where(first, features, crossed), jnp.where(first, crossed, features)], axis=1
    )

    total = partial[0]
    for d in range(1, NX):
        total = total + along_x(sent[d], -d).astype(f32)
    low_rank = total.astype(bf16)

    low_rank, pieces[1] = lax.optimization_barrier((low_rank, pieces[1]))
    low = jnp.concatenate([low_rank] + [along_y(low_rank, d) for d in range(1, NY)], axis=0)

    for slot, o in zip(slots, sources):
        slot.append(fetch(pieces[1], o))

    weights, low = lax.optimization_barrier((weights[0], low))
    kept = jnp.concatenate([columns(weights, at, quarter) for at in here_at], axis=1)
    given = jnp.concatenate([columns(weights, at, quarter) for at in there_at], axis=1)
    old = jnp.zeros((NY * 16, 2 * quarter), bf16)
    old = put(old, kept, y * 16, 0)
    for d in range(1, NY):
        old = put(old, along_y(given if d % 2 else kept, d), lax.rem(y + NY - d, NY) * 16, 0)

    projected = dot(features.reshape(-1, NY * tokens), low, ((1,), (0,)))
    projected = projected.astype(bf16).reshape(2 * NX * NZ, 16, half)
    got = lax.all_to_all(projected, ("dp", "tensor"), split_axis=0, concat_axis=0, tiled=True)
    got = got.reshape(NX * NZ, 2, 16, half).astype(f32).sum(axis=0)
    projected = jnp.concatenate([got[0], got[1]], axis=1)[None]

    first_new = beta_one * first_moment + (1.0 - beta_one) * projected
    second_new = beta_two * second_moment + (1.0 - beta_two) * projected * projected
    corrected = first_new / (1.0 - beta_one**STEP)
    scaled = jnp.sqrt(second_new / (1.0 - beta_two**STEP)) + epsilon
    direction = (corrected / scaled).astype(bf16)[0]

    halves = jnp.stack([direction[:, :half], direction[:, half:]])
    directions = lax.all_to_all(
        jnp.broadcast_to(halves[None], (NY, 2, 16, half)).reshape(NY * 2, 16, half),
        ("fsdp", "tensor"),
        split_axis=0,
        concat_axis=0,
        tiled=True,
    )
    directions = directions.reshape(NY, 2, 16, half).transpose(1, 0, 2, 3).reshape(2, NY * 16, half)
    new_weights = jnp.zeros((NY * 16, width), bf16)
    stacked = directions.reshape(-1, half)
    both = [dot(stacked, piece, ((1,), (1,))) for slot in slots for piece in slot]
    both = jnp.concatenate(both, axis=1).reshape(2, NY * 16, 2 * quarter)
    ours, theirs = jnp.where(first, both[0], both[1]), jnp.where(first, both[1], both[0])
    update = ours + across(theirs.astype(bf16)).astype(f32)
    done = (old.astype(f32) - step_scale * update).astype(bf16)
    for n, turn in enumerate((-1, 1)):
        part = done[:, n * quarter : (n + 1) * quarter]
        new_weights = put(new_weights, part, here_at[n], 1)
        new_weights = put(new_weights, along_y(part, turn), there_at[n], 1)
    return (new_weights[None], first_new, second_new)


def solution(mesh):
    return jax.shard_map(
        shards,
        mesh=mesh,
        in_specs=(
            P(("dp", "fsdp"), None),
            P(("dp", "fsdp"), "tensor", None),
            P("dp", None),
            P("tensor", ("dp", "fsdp"), None),
            P("tensor", ("dp", "fsdp"), None),
            P("tensor", ("dp", "fsdp"), None),
        ),
        out_specs=(
            P("tensor", "dp", None),
            P("tensor", ("dp", "fsdp"), None),
            P("tensor", ("dp", "fsdp"), None),
        ),
        check_vma=False,
    )
```

```python
import jax
import jax.numpy as jnp
from jax import lax
from jax.experimental import pallas as pl
from jax.experimental.pallas import tpu as pltpu
from jax.sharding import PartitionSpec as P

STEP = 10

beta_one = 0.9
beta_two = 0.999
epsilon = 1e-08
step_scale = 0.25

NX, NZ, NY = 4, 8, 4
FAR = (2, 1, 3)
f32 = jnp.float32
bf16 = jnp.bfloat16


def along_x(value, d):
    pairs = [(x * NZ + z, (x + d) % NX * NZ + z) for x in range(NX) for z in range(NZ)]
    return lax.ppermute(value, "dp", pairs)


def along_z(value, d):
    pairs = [(x * NZ + z, x * NZ + (z + d) % NZ) for x in range(NX) for z in range(NZ)]
    return lax.ppermute(value, "dp", pairs)


def along_y(value, d):
    return lax.ppermute(value, "fsdp", [(y, (y + d) % NY) for y in range(NY)])


def across(value):
    return lax.ppermute(value, "tensor", [(0, 1), (1, 0)])


def rows(array, start, size):
    return lax.dynamic_slice_in_dim(array, start, size, axis=0)


def columns(array, start, size):
    return lax.dynamic_slice_in_dim(array, start, size, axis=1)


def put(whole, part, start, axis):
    return lax.dynamic_update_slice_in_dim(whole, part, start, axis=axis)


def gather_y(block, y):
    n = block.shape[0]
    whole = jnp.zeros((NY * n, block.shape[1]), block.dtype)
    whole = put(whole, block, y * n, 0)
    for d in range(1, NY):
        whole = put(whole, along_y(block, d), lax.rem(y + NY - d, NY) * n, 0)
    return whole


def dot(a, b, dims):
    return lax.dot_general(a, b, ((dims[0], dims[1]), ((), ())), preferred_element_type=f32)


def cut(activations, places):
    pair, quarter = activations.shape[0] // 2, activations.shape[1] // NX

    def kernel(act_ref, *refs):
        outs, sems = refs[:-1], refs[-1]
        core, x = lax.axis_index("tensor"), lax.div(lax.axis_index("dp"), NZ)
        copies = []
        for n, (out, (other, d)) in enumerate(zip(outs, places)):
            row = pl.multiple_of((1 - core if other else core) * pair, pair)
            col = pl.multiple_of(lax.rem(x + d, NX) * quarter, quarter)
            source = act_ref.at[pl.ds(row, pair), pl.ds(col, quarter)]
            copies.append(pltpu.make_async_copy(source, out, sems.at[n]))
        for copy in copies:
            copy.start()
        for copy in copies:
            copy.wait()

    shape = jax.ShapeDtypeStruct((pair, quarter), activations.dtype)
    return pl.pallas_call(
        kernel,
        out_shape=[shape] * len(places),
        in_specs=[pl.BlockSpec(memory_space=pl.ANY)],
        out_specs=[pl.BlockSpec(memory_space=pltpu.VMEM)] * len(places),
        scratch_shapes=[pltpu.SemaphoreType.DMA((len(places),))],
    )(activations)


def cut_weights(weights):
    count, width = weights.shape
    quarter, slab = width // NX, width // NX // NY

    def kernel(weights_ref, *refs):
        outs, sems = refs[:-1], refs[-1]
        x, y = lax.div(lax.axis_index("dp"), NZ), lax.axis_index("fsdp")
        copies = []
        for n, (out, e) in enumerate(zip(outs, (0,) + FAR)):
            for k, d in enumerate((0,) + FAR):
                col = lax.rem(x + NX - d, NX) * quarter + lax.rem(y + e, NY) * slab
                source = weights_ref.at[:, pl.ds(pl.multiple_of(col, slab), slab)]
                target = out.at[:, pl.ds(k * slab, slab)]
                copies.append(pltpu.make_async_copy(source, target, sems.at[n, k]))
        for copy in copies:
            copy.start()
        for copy in copies:
            copy.wait()

    shape = jax.ShapeDtypeStruct((count, quarter), weights.dtype)
    return pl.pallas_call(
        kernel,
        out_shape=[shape] * NY,
        in_specs=[pl.BlockSpec(memory_space=pl.ANY)],
        out_specs=[pl.BlockSpec(memory_space=pltpu.VMEM)] * NY,
        scratch_shapes=[pltpu.SemaphoreType.DMA((NY, NX))],
    )(weights)


def place(parts):
    count, quarter = parts[0].shape
    slab = quarter // NY

    def kernel(*refs):
        ins, out = refs[:-1], refs[-1]
        x, y = lax.div(lax.axis_index("dp"), NZ), lax.axis_index("fsdp")
        for part, e in zip(ins, (0,) + FAR):
            for k, d in enumerate((0,) + FAR):
                col = lax.rem(x + NX - d, NX) * quarter + lax.rem(y + NY - e, NY) * slab
                out[:, pl.ds(pl.multiple_of(col, slab), slab)] = part[:, k * slab : (k + 1) * slab]

    return pl.pallas_call(
        kernel,
        out_shape=jax.ShapeDtypeStruct((count, quarter * NX), parts[0].dtype),
        in_specs=[pl.BlockSpec(memory_space=pltpu.VMEM)] * NY,
        out_specs=pl.BlockSpec(memory_space=pltpu.VMEM),
    )(*parts)


def shards(activations, out_grads, basis, weights, first_moment, second_moment):
    dp, y, core = lax.axis_index("dp"), lax.axis_index("fsdp"), lax.axis_index("tensor")
    x, z = lax.div(dp, NZ), lax.rem(dp, NZ)
    tokens, width = activations.shape
    rank = basis.shape[1]
    half, quarter, pair = rank // 2, width // NX, tokens // 2

    mine = columns(basis, core * half, half)
    n = mine.shape[0]
    ahead, back = along_z(mine, 1), along_z(mine, -1)
    here, there, *leaving = cut(activations, [(False, 0), (True, 0)] + [(False, d) for d in FAR])
    ahead, back, leaving = lax.optimization_barrier((ahead, back, leaving))
    own = [along_x(piece, d) for d, piece in zip(FAR, leaving)]

    held = jnp.zeros((NZ * n, half), bf16)
    held = put(held, mine, z * n, 0)
    for s in range(1, NZ // 2):
        if s > 1:
            ahead, back = along_z(ahead, 1), along_z(back, -1)
        held = put(held, ahead, lax.rem(z + NZ - s, NZ) * n, 0)
        held = put(held, back, lax.rem(z + s, NZ) * n, 0)
    back, out_grads = lax.optimization_barrier((back, out_grads))
    turned = out_grads[:, 0, :].T.reshape(NX * NZ, NY, 16, tokens)
    parts = []
    for d in (0,) + FAR:
        part = lax.dynamic_index_in_dim(turned, lax.rem(y + d, NY), axis=1, keepdims=False)
        parts.append(part if d == 0 else along_y(part, d))

    own, _, parts = lax.optimization_barrier((own, back, parts))
    back, activations = lax.optimization_barrier((back, activations))

    far = lax.rem(z + NZ // 2, NZ) * n
    held = put(held, along_z(ahead, 1), far, 0)
    other = [there] + [across(piece) for piece in own]
    own = [here] + own

    first = core == 0
    near = dot(jnp.concatenate(own, axis=0), held, ((1,), (0,))).reshape(NX, pair, half)
    away = dot(jnp.concatenate(other, axis=0), held, ((1,), (0,))).reshape(NX, pair, half)
    partial = jnp.concatenate(
        [jnp.where(first, near, away), jnp.where(first, away, near)], axis=1
    )
    sent = partial.astype(bf16)
    features = jnp.concatenate(parts, axis=2)
    crossed = across(features)
    features = jnp.stack(
        [jnp.where(first, features, crossed), jnp.where(first, crossed, features)], axis=1
    )

    total = partial[0]
    for n, d in enumerate(FAR, 1):
        total = total + along_x(sent[n], -d).astype(f32)
    low_rank = total.astype(bf16)

    low_rank, held = lax.optimization_barrier((low_rank, held))
    slab = quarter // NY
    piece = rows(held, y * slab, slab)
    kept = jnp.concatenate([piece] + [along_x(piece, d) for d in FAR], axis=0)
    low = jnp.concatenate([low_rank] + [along_y(low_rank, d) for d in FAR], axis=0)

    weights, low = lax.optimization_barrier((weights[0], low))
    mine, *leaving = cut_weights(weights)
    old = put(jnp.zeros((NY * 16, quarter), bf16), mine, y * 16, 0)
    for d, piece in zip(FAR, leaving):
        old = put(old, along_y(piece, d), lax.rem(y + NY - d, NY) * 16, 0)

    projected = dot(features.reshape(-1, NY * tokens), low, ((1,), (0,)))
    projected = projected.astype(bf16).reshape(2 * NX * NZ, 16, half)
    got = lax.all_to_all(projected, ("dp", "tensor"), split_axis=0, concat_axis=0, tiled=True)
    got = got.reshape(NX * NZ, 2, 16, half).astype(f32).sum(axis=0)
    projected = jnp.concatenate([got[0], got[1]], axis=1)[None]

    first_new = beta_one * first_moment + (1.0 - beta_one) * projected
    second_new = beta_two * second_moment + (1.0 - beta_two) * projected * projected
    corrected = first_new / (1.0 - beta_one**STEP)
    scaled = jnp.sqrt(second_new / (1.0 - beta_two**STEP)) + epsilon
    direction = (corrected / scaled).astype(bf16)[0]

    halves = jnp.stack([direction[:, :half], direction[:, half:]])
    directions = lax.all_to_all(
        jnp.broadcast_to(halves[None], (NY, 2, 16, half)).reshape(NY * 2, 16, half),
        ("fsdp", "tensor"),
        split_axis=0,
        concat_axis=0,
        tiled=True,
    )
    directions = directions.reshape(NY, 2, 16, half).transpose(1, 0, 2, 3).reshape(2, NY * 16, half)
    both = dot(directions.reshape(-1, half), kept, ((1,), (1,))).reshape(2, NY * 16, quarter)
    ours, theirs = jnp.where(first, both[0], both[1]), jnp.where(first, both[1], both[0])
    update = ours + across(theirs.astype(bf16)).astype(f32)
    done = (old.astype(f32) - step_scale * update).astype(bf16)
    new_weights = place([done] + [along_y(done, d) for d in FAR])
    return (new_weights[None], first_new, second_new)


def solution(mesh):
    return jax.shard_map(
        shards,
        mesh=mesh,
        in_specs=(
            P(("dp", "fsdp"), None),
            P(("dp", "fsdp"), "tensor", None),
            P("dp", None),
            P("tensor", ("dp", "fsdp"), None),
            P("tensor", ("dp", "fsdp"), None),
            P("tensor", ("dp", "fsdp"), None),
        ),
        out_specs=(
            P("tensor", "dp", None),
            P("tensor", ("dp", "fsdp"), None),
            P("tensor", ("dp", "fsdp"), None),
        ),
        check_vma=False,
    )
```

```python
import jax
import jax.numpy as jnp
from jax import lax
from jax.experimental import pallas as pl
from jax.experimental.pallas import tpu as pltpu
from jax.sharding import PartitionSpec as P

STEP = 10

beta_one = 0.9
beta_two = 0.999
epsilon = 1e-08
step_scale = 0.25

NX, NZ, NY = 4, 8, 4
FAR = (2, 1, 3)
f32 = jnp.float32
bf16 = jnp.bfloat16


def along_x(value, d):
    pairs = [(x * NZ + z, (x + d) % NX * NZ + z) for x in range(NX) for z in range(NZ)]
    return lax.ppermute(value, "dp", pairs)


def along_z(value, d):
    pairs = [(x * NZ + z, x * NZ + (z + d) % NZ) for x in range(NX) for z in range(NZ)]
    return lax.ppermute(value, "dp", pairs)


def along_y(value, d):
    return lax.ppermute(value, "fsdp", [(y, (y + d) % NY) for y in range(NY)])


def across(value):
    return lax.ppermute(value, "tensor", [(0, 1), (1, 0)])


def rows(array, start, size):
    return lax.dynamic_slice_in_dim(array, start, size, axis=0)


def columns(array, start, size):
    return lax.dynamic_slice_in_dim(array, start, size, axis=1)


def put(whole, part, start, axis):
    return lax.dynamic_update_slice_in_dim(whole, part, start, axis=axis)


def gather_y(block, y):
    n = block.shape[0]
    whole = jnp.zeros((NY * n, block.shape[1]), block.dtype)
    whole = put(whole, block, y * n, 0)
    for d in range(1, NY):
        whole = put(whole, along_y(block, d), lax.rem(y + NY - d, NY) * n, 0)
    return whole


def dot(a, b, dims):
    return lax.dot_general(a, b, ((dims[0], dims[1]), ((), ())), preferred_element_type=f32)


def cut(activations, places):
    pair, quarter = activations.shape[0] // 2, activations.shape[1] // NX

    def kernel(act_ref, *refs):
        outs, sems = refs[:-1], refs[-1]
        core, x = lax.axis_index("tensor"), lax.div(lax.axis_index("dp"), NZ)
        copies = []
        for n, (out, (other, d)) in enumerate(zip(outs, places)):
            row = pl.multiple_of((1 - core if other else core) * pair, pair)
            col = pl.multiple_of(lax.rem(x + d, NX) * quarter, quarter)
            source = act_ref.at[pl.ds(row, pair), pl.ds(col, quarter)]
            copies.append(pltpu.make_async_copy(source, out, sems.at[n]))
        for copy in copies:
            copy.start()
        for copy in copies:
            copy.wait()

    shape = jax.ShapeDtypeStruct((pair, quarter), activations.dtype)
    return pl.pallas_call(
        kernel,
        out_shape=[shape] * len(places),
        in_specs=[pl.BlockSpec(memory_space=pl.ANY)],
        out_specs=[pl.BlockSpec(memory_space=pltpu.VMEM)] * len(places),
        scratch_shapes=[pltpu.SemaphoreType.DMA((len(places),))],
    )(activations)


def cut_weights(weights):
    count, width = weights.shape
    quarter, slab = width // NX, width // NX // NY

    def kernel(weights_ref, *refs):
        outs, sems = refs[:-1], refs[-1]
        x, y = lax.div(lax.axis_index("dp"), NZ), lax.axis_index("fsdp")
        copies = []
        for n, (out, e) in enumerate(zip(outs, (0,) + FAR)):
            for k, d in enumerate((0,) + FAR):
                col = lax.rem(x + NX - d, NX) * quarter + lax.rem(y + e, NY) * slab
                source = weights_ref.at[:, pl.ds(pl.multiple_of(col, slab), slab)]
                target = out.at[:, pl.ds(k * slab, slab)]
                copies.append(pltpu.make_async_copy(source, target, sems.at[n, k]))
        for copy in copies:
            copy.start()
        for copy in copies:
            copy.wait()

    shape = jax.ShapeDtypeStruct((count, quarter), weights.dtype)
    return pl.pallas_call(
        kernel,
        out_shape=[shape] * NY,
        in_specs=[pl.BlockSpec(memory_space=pl.ANY)],
        out_specs=[pl.BlockSpec(memory_space=pltpu.VMEM)] * NY,
        scratch_shapes=[pltpu.SemaphoreType.DMA((NY, NX))],
    )(weights)


def shards(activations, out_grads, basis, weights, first_moment, second_moment):
    dp, y, core = lax.axis_index("dp"), lax.axis_index("fsdp"), lax.axis_index("tensor")
    x, z = lax.div(dp, NZ), lax.rem(dp, NZ)
    tokens, width = activations.shape
    rank = basis.shape[1]
    half, quarter, pair = rank // 2, width // NX, tokens // 2

    mine = columns(basis, core * half, half)
    n = mine.shape[0]
    ahead, back = along_z(mine, 1), along_z(mine, -1)
    here, there, *leaving = cut(activations, [(False, 0), (True, 0)] + [(False, d) for d in FAR])
    ahead, back, leaving = lax.optimization_barrier((ahead, back, leaving))
    own = [along_x(piece, d) for d, piece in zip(FAR, leaving)]

    held = jnp.zeros((NZ * n, half), bf16)
    held = put(held, mine, z * n, 0)
    for s in range(1, NZ // 2):
        if s > 1:
            ahead, back = along_z(ahead, 1), along_z(back, -1)
        held = put(held, ahead, lax.rem(z + NZ - s, NZ) * n, 0)
        held = put(held, back, lax.rem(z + s, NZ) * n, 0)
    back, out_grads = lax.optimization_barrier((back, out_grads))
    turned = out_grads[:, 0, :].T.reshape(NX * NZ, NY, 16, tokens)
    parts = []
    for d in (0,) + FAR:
        part = lax.dynamic_index_in_dim(turned, lax.rem(y + d, NY), axis=1, keepdims=False)
        parts.append(part if d == 0 else along_y(part, d))

    own, _, parts = lax.optimization_barrier((own, back, parts))
    back, activations = lax.optimization_barrier((back, activations))

    far = lax.rem(z + NZ // 2, NZ) * n
    held = put(held, along_z(ahead, 1), far, 0)
    other = [there] + [across(piece) for piece in own]
    own = [here] + own

    first = core == 0
    near = dot(jnp.concatenate(own, axis=0), held, ((1,), (0,))).reshape(NX, pair, half)
    away = dot(jnp.concatenate(other, axis=0), held, ((1,), (0,))).reshape(NX, pair, half)
    partial = jnp.concatenate(
        [jnp.where(first, near, away), jnp.where(first, away, near)], axis=1
    )
    sent = partial.astype(bf16)
    features = jnp.concatenate(parts, axis=2)
    crossed = across(features)
    features = jnp.stack(
        [jnp.where(first, features, crossed), jnp.where(first, crossed, features)], axis=1
    )

    total = partial[0]
    for n, d in enumerate(FAR, 1):
        total = total + along_x(sent[n], -d).astype(f32)
    low_rank = total.astype(bf16)

    low_rank, held = lax.optimization_barrier((low_rank, held))
    slab = quarter // NY
    piece = rows(held, y * slab, slab)
    kept = jnp.concatenate([piece] + [along_x(piece, d) for d in FAR], axis=0)
    low = jnp.concatenate([low_rank] + [along_y(low_rank, d) for d in FAR], axis=0)

    weights, low = lax.optimization_barrier((weights[0], low))
    mine, *leaving = cut_weights(weights)
    old = put(jnp.zeros((NY * 16, quarter), bf16), mine, y * 16, 0)
    for d, piece in zip(FAR, leaving):
        old = put(old, along_y(piece, d), lax.rem(y + NY - d, NY) * 16, 0)

    projected = dot(features.reshape(-1, NY * tokens), low, ((1,), (0,)))
    projected = projected.astype(bf16).reshape(2 * NX * NZ, 16, half)
    got = lax.all_to_all(projected, ("dp", "tensor"), split_axis=0, concat_axis=0, tiled=True)
    got = got.reshape(NX * NZ, 2, 16, half).astype(f32).sum(axis=0)
    projected = jnp.concatenate([got[0], got[1]], axis=1)[None]

    first_new = beta_one * first_moment + (1.0 - beta_one) * projected
    second_new = beta_two * second_moment + (1.0 - beta_two) * projected * projected
    corrected = first_new / (1.0 - beta_one**STEP)
    scaled = jnp.sqrt(second_new / (1.0 - beta_two**STEP)) + epsilon
    direction = (corrected / scaled).astype(bf16)[0]

    halves = jnp.stack([direction[:, :half], direction[:, half:]])
    directions = lax.all_to_all(
        jnp.broadcast_to(halves[None], (NY, 2, 16, half)).reshape(NY * 2, 16, half),
        ("fsdp", "tensor"),
        split_axis=0,
        concat_axis=0,
        tiled=True,
    )
    directions = directions.reshape(NY, 2, 16, half).transpose(1, 0, 2, 3).reshape(2, NY * 16, half)
    both = dot(directions.reshape(-1, half), kept, ((1,), (1,))).reshape(2, NY * 16, quarter)
    ours, theirs = jnp.where(first, both[0], both[1]), jnp.where(first, both[1], both[0])
    update = ours + across(theirs.astype(bf16)).astype(f32)
    done = (old.astype(f32) - step_scale * update).astype(bf16)
    new_weights = jnp.zeros((NY * 16, width), bf16)
    for e in (0,) + FAR:
        part = along_y(done, e) if e else done
        for k, d in enumerate((0,) + FAR):
            at = lax.rem(x + NX - d, NX) * quarter + lax.rem(y + NY - e, NY) * slab
            new_weights = put(new_weights, part[:, k * slab : (k + 1) * slab], at, 1)
    return (new_weights[None], first_new, second_new)


def solution(mesh):
    return jax.shard_map(
        shards,
        mesh=mesh,
        in_specs=(
            P(("dp", "fsdp"), None),
            P(("dp", "fsdp"), "tensor", None),
            P("dp", None),
            P("tensor", ("dp", "fsdp"), None),
            P("tensor", ("dp", "fsdp"), None),
            P("tensor", ("dp", "fsdp"), None),
        ),
        out_specs=(
            P("tensor", "dp", None),
            P("tensor", ("dp", "fsdp"), None),
            P("tensor", ("dp", "fsdp"), None),
        ),
        check_vma=False,
    )
```

```python
import jax
import jax.numpy as jnp
from jax import lax
from jax.experimental import pallas as pl
from jax.experimental.pallas import tpu as pltpu
from jax.sharding import PartitionSpec as P

STEP = 10

beta_one = 0.9
beta_two = 0.999
epsilon = 1e-08
step_scale = 0.25

NX, NZ, NY = 4, 8, 4
FAR = (2, 1, 3)
f32 = jnp.float32
bf16 = jnp.bfloat16


def along_x(value, d):
    pairs = [(x * NZ + z, (x + d) % NX * NZ + z) for x in range(NX) for z in range(NZ)]
    return lax.ppermute(value, "dp", pairs)


def along_z(value, d):
    pairs = [(x * NZ + z, x * NZ + (z + d) % NZ) for x in range(NX) for z in range(NZ)]
    return lax.ppermute(value, "dp", pairs)


def along_y(value, d):
    return lax.ppermute(value, "fsdp", [(y, (y + d) % NY) for y in range(NY)])


def across(value):
    return lax.ppermute(value, "tensor", [(0, 1), (1, 0)])


def rows(array, start, size):
    return lax.dynamic_slice_in_dim(array, start, size, axis=0)


def columns(array, start, size):
    return lax.dynamic_slice_in_dim(array, start, size, axis=1)


def put(whole, part, start, axis):
    return lax.dynamic_update_slice_in_dim(whole, part, start, axis=axis)


def gather_y(block, y):
    n = block.shape[0]
    whole = jnp.zeros((NY * n, block.shape[1]), block.dtype)
    whole = put(whole, block, y * n, 0)
    for d in range(1, NY):
        whole = put(whole, along_y(block, d), lax.rem(y + NY - d, NY) * n, 0)
    return whole


def dot(a, b, dims):
    return lax.dot_general(a, b, ((dims[0], dims[1]), ((), ())), preferred_element_type=f32)


def cut(activations, places):
    pair, quarter = activations.shape[0] // 2, activations.shape[1] // NX

    def kernel(act_ref, *refs):
        outs, sems = refs[:-1], refs[-1]
        core, x = lax.axis_index("tensor"), lax.div(lax.axis_index("dp"), NZ)
        copies = []
        for n, (out, (other, d)) in enumerate(zip(outs, places)):
            row = pl.multiple_of((1 - core if other else core) * pair, pair)
            col = pl.multiple_of(lax.rem(x + d, NX) * quarter, quarter)
            source = act_ref.at[pl.ds(row, pair), pl.ds(col, quarter)]
            copies.append(pltpu.make_async_copy(source, out, sems.at[n]))
        for copy in copies:
            copy.start()
        for copy in copies:
            copy.wait()

    shape = jax.ShapeDtypeStruct((pair, quarter), activations.dtype)
    return pl.pallas_call(
        kernel,
        out_shape=[shape] * len(places),
        in_specs=[pl.BlockSpec(memory_space=pl.ANY)],
        out_specs=[pl.BlockSpec(memory_space=pltpu.VMEM)] * len(places),
        scratch_shapes=[pltpu.SemaphoreType.DMA((len(places),))],
    )(activations)


def cut_weights(weights):
    count, width = weights.shape
    quarter, slab = width // NX, width // NX // NY

    def kernel(weights_ref, *refs):
        outs, sems = refs[:-1], refs[-1]
        x, y = lax.div(lax.axis_index("dp"), NZ), lax.axis_index("fsdp")
        copies = []
        for n, (out, e) in enumerate(zip(outs, (0,) + FAR)):
            for k, d in enumerate((0,) + FAR):
                col = lax.rem(x + NX - d, NX) * quarter + lax.rem(y + e, NY) * slab
                source = weights_ref.at[:, pl.ds(pl.multiple_of(col, slab), slab)]
                target = out.at[:, pl.ds(k * slab, slab)]
                copies.append(pltpu.make_async_copy(source, target, sems.at[n, k]))
        for copy in copies:
            copy.start()
        for copy in copies:
            copy.wait()

    shape = jax.ShapeDtypeStruct((count, quarter), weights.dtype)
    return pl.pallas_call(
        kernel,
        out_shape=[shape] * NY,
        in_specs=[pl.BlockSpec(memory_space=pl.ANY)],
        out_specs=[pl.BlockSpec(memory_space=pltpu.VMEM)] * NY,
        scratch_shapes=[pltpu.SemaphoreType.DMA((NY, NX))],
    )(weights)


def shards(activations, out_grads, basis, weights, first_moment, second_moment):
    dp, y, core = lax.axis_index("dp"), lax.axis_index("fsdp"), lax.axis_index("tensor")
    x, z = lax.div(dp, NZ), lax.rem(dp, NZ)
    tokens, width = activations.shape
    rank = basis.shape[1]
    half, quarter, pair = rank // 2, width // NX, tokens // 2

    mine = columns(basis, core * half, half)
    n = mine.shape[0]
    ahead, back = along_z(mine, 1), along_z(mine, -1)
    here, there, *leaving = cut(activations, [(False, 0), (True, 0)] + [(False, d) for d in FAR])
    ahead, back, leaving = lax.optimization_barrier((ahead, back, leaving))
    own = [along_x(piece, d) for d, piece in zip(FAR, leaving)]

    held = jnp.zeros((NZ * n, half), bf16)
    held = put(held, mine, z * n, 0)
    for s in range(1, NZ // 2):
        if s > 1:
            ahead, back = along_z(ahead, 1), along_z(back, -1)
        held = put(held, ahead, lax.rem(z + NZ - s, NZ) * n, 0)
        held = put(held, back, lax.rem(z + s, NZ) * n, 0)
    back, out_grads = lax.optimization_barrier((back, out_grads))
    turned = out_grads[:, 0, :].T.reshape(NX * NZ, NY, 16, tokens)
    parts = []
    for d in (0,) + FAR:
        part = lax.dynamic_index_in_dim(turned, lax.rem(y + d, NY), axis=1, keepdims=False)
        parts.append(part if d == 0 else along_y(part, d))

    own, _, parts = lax.optimization_barrier((own, back, parts))
    back, activations = lax.optimization_barrier((back, activations))

    far = lax.rem(z + NZ // 2, NZ) * n
    held = put(held, along_z(ahead, 1), far, 0)
    other = [there] + [across(piece) for piece in own]
    own = [here] + own

    first = core == 0
    near = dot(jnp.concatenate(own, axis=0), held, ((1,), (0,))).reshape(NX, pair, half)
    away = dot(jnp.concatenate(other, axis=0), held, ((1,), (0,))).reshape(NX, pair, half)
    partial = jnp.concatenate(
        [jnp.where(first, near, away), jnp.where(first, away, near)], axis=1
    )
    sent = partial.astype(bf16)
    features = jnp.concatenate(parts, axis=2)
    crossed = across(features)
    features = jnp.stack(
        [jnp.where(first, features, crossed), jnp.where(first, crossed, features)], axis=1
    )

    total = partial[0]
    for n, d in enumerate(FAR, 1):
        total = total + along_x(sent[n], -d).astype(f32)
    low_rank = total.astype(bf16)

    low_rank, held = lax.optimization_barrier((low_rank, held))
    slab = quarter // NY
    piece = rows(held, y * slab, slab)
    kept = [piece] + [along_x(piece, d) for d in FAR]
    low = jnp.concatenate([low_rank] + [along_y(low_rank, d) for d in FAR], axis=0)

    weights, low_rank_ = lax.optimization_barrier((weights[0], low_rank))
    mine, *leaving = cut_weights(weights)
    old = put(jnp.zeros((NY * 16, quarter), bf16), mine, y * 16, 0)
    for d, piece in zip(FAR, leaving):
        old = put(old, along_y(piece, d), lax.rem(y + NY - d, NY) * 16, 0)

    projected = dot(features.reshape(-1, NY * tokens), low, ((1,), (0,)))
    projected = projected.astype(bf16).reshape(2 * NX * NZ, 16, half)
    got = lax.all_to_all(projected, ("dp", "tensor"), split_axis=0, concat_axis=0, tiled=True)
    got, old = lax.optimization_barrier((got, old))
    got = got.reshape(NX * NZ, 2, 16, half).astype(f32).sum(axis=0)
    projected = jnp.concatenate([got[0], got[1]], axis=1)[None]

    first_new = beta_one * first_moment + (1.0 - beta_one) * projected
    second_new = beta_two * second_moment + (1.0 - beta_two) * projected * projected
    corrected = first_new / (1.0 - beta_one**STEP)
    scaled = jnp.sqrt(second_new / (1.0 - beta_two**STEP)) + epsilon
    direction = (corrected / scaled).astype(bf16)[0]

    halves = jnp.stack([direction[:, :half], direction[:, half:]])
    directions = lax.all_to_all(
        jnp.broadcast_to(halves[None], (NY, 2, 16, half)).reshape(NY * 2, 16, half),
        ("fsdp", "tensor"),
        split_axis=0,
        concat_axis=0,
        tiled=True,
    )
    directions = directions.reshape(NY, 2, 16, half).transpose(1, 0, 2, 3).reshape(2, NY * 16, half)
    stacked = directions.reshape(-1, half)
    both = jnp.concatenate([dot(stacked, part, ((1,), (1,))) for part in kept], axis=1)
    both = both.reshape(2, NY * 16, quarter)
    ours, theirs = jnp.where(first, both[0], both[1]), jnp.where(first, both[1], both[0])
    update = ours + across(theirs.astype(bf16)).astype(f32)
    done = (old.astype(f32) - step_scale * update).astype(bf16)
    new_weights = jnp.zeros((NY * 16, width), bf16)
    for e in (0,) + FAR:
        part = along_y(done, e) if e else done
        for k, d in enumerate((0,) + FAR):
            at = lax.rem(x + NX - d, NX) * quarter + lax.rem(y + NY - e, NY) * slab
            new_weights = put(new_weights, part[:, k * slab : (k + 1) * slab], at, 1)
    return (new_weights[None], first_new, second_new)


def solution(mesh):
    return jax.shard_map(
        shards,
        mesh=mesh,
        in_specs=(
            P(("dp", "fsdp"), None),
            P(("dp", "fsdp"), "tensor", None),
            P("dp", None),
            P("tensor", ("dp", "fsdp"), None),
            P("tensor", ("dp", "fsdp"), None),
            P("tensor", ("dp", "fsdp"), None),
        ),
        out_specs=(
            P("tensor", "dp", None),
            P("tensor", ("dp", "fsdp"), None),
            P("tensor", ("dp", "fsdp"), None),
        ),
        check_vma=False,
    )
```
